128 devices in a mesh: seq: 32 (over x, y, core), head: 4 (over z).
Axes of the slice: x: 4, y: 4, z: 4, core: 2. Of those that a mesh axis runs over, the one named last changes fastest.
Arguments:
- queries: bfloat16 [65536, 4096], P('seq', 'head'), may hold values from -8 to 8
- keys: bfloat16 [65536, 4096], P('seq', 'head'), may hold values from -8 to 8
- values: bfloat16 [65536, 4096], P('seq', 'head'), may hold values from -10 to 10
- gain: float32 [4096], P('head'), may hold values from 0.5 to 1.5
Outputs:
- mixed: bfloat16 [65536, 4096], P('seq', 'head')
The draws below stay inside these ranges and needn't reach their ends.
All inputs are finite; a program needn't handle non-finite values.
Results may differ from the reference program's by a relative error of at most 0.034.
Values may be sent and summed in bfloat16 or wider, within the bound.
No kernel may reach another device: no remote copies, remote signals or barrier semaphores. Data moves between devices by JAX's collectives and lax.ppermute only.
A program may use at most 192 MiB of HBM per device.

```python
import math
import jax
import jax.numpy as jnp
from jax import lax

HEADS = 32
HEAD_DIM = 128
BLOCK = 128
TOKENS = 65536


def draw_queries(key, part):
    key = jax.random.fold_in(key, 1)
    field = jax.random.normal(key, (TOKENS, HEADS, HEAD_DIM))
    return field.reshape(TOKENS, HEADS * HEAD_DIM).astype(jnp.bfloat16)


def draw_keys(key, part):
    key = jax.random.fold_in(key, 2)
    field = jax.random.normal(key, (TOKENS, HEADS, HEAD_DIM))
    return field.reshape(TOKENS, HEADS * HEAD_DIM).astype(jnp.bfloat16)


def draw_values(key, part):
    key = jax.random.fold_in(key, 3)
    position = jnp.arange(HEADS, dtype=jnp.float32) / (HEADS - 1)
    ramp = 0.5 * jnp.exp(position * 1.0986)
    noise = jnp.clip(jax.random.normal(key, (TOKENS, HEADS, HEAD_DIM)), -6.0, 6.0)
    field = noise * ramp[None, :, None]
    return field.reshape(TOKENS, HEADS * HEAD_DIM).astype(jnp.bfloat16)


def setup_inputs(seed: int = 0) -> dict:
    streams_of = jax.random.split(jax.random.key(seed), 5)
    queries = draw_queries(jax.random.fold_in(streams_of[4], 71), 0)
    keys = draw_keys(jax.random.fold_in(streams_of[4], 71), 0)
    values = draw_values(jax.random.fold_in(streams_of[4], 71), 0)
    gain = jnp.clip(1.0 + 0.1 * jax.random.normal(streams_of[3], (HEADS * HEAD_DIM,), jnp.float32), 0.5, 1.5)
    return {"queries": queries, "keys": keys, "values": values, "gain": gain}


def halve_rows(tensor):
    split_shape = (tensor.shape[0] // 2, 2) + tensor.shape[1:]
    return (lax.optimization_barrier(jnp.sum(tensor.reshape(split_shape).astype(jnp.float32), axis=1)) * 0.5).astype(jnp.bfloat16)

def attend(level_queries, level_keys, level_values):
    score_scale = 1.0 / math.sqrt(HEAD_DIM)
    scores = jnp.einsum('grd,gkd->grk', level_queries.astype(jnp.float32), level_keys.astype(jnp.float32)) * score_scale
    maxima = lax.optimization_barrier(jnp.max(scores, axis=-1))
    weights = jnp.exp(scores - maxima[..., None])
    totals = lax.optimization_barrier(jnp.sum(weights, axis=-1))
    rounded = lax.optimization_barrier(weights.astype(jnp.bfloat16))
    weighted = jnp.einsum('grk,gkd->grd', rounded.astype(jnp.float32), level_values.astype(jnp.float32))
    return (maxima, totals, weighted)

def head_layer(head_arrays):
    head_queries, head_keys, head_values = head_arrays
    seq_len = head_queries.shape[0]
    level_total = (seq_len // BLOCK).bit_length() - 1
    group_count = seq_len // (2 * BLOCK)
    maxima, totals, weighted = attend(head_queries.reshape(group_count, 2 * BLOCK, HEAD_DIM), head_keys.reshape(group_count, 2 * BLOCK, HEAD_DIM), head_values.reshape(group_count, 2 * BLOCK, HEAD_DIM))
    results = [(maxima.reshape(seq_len), totals.reshape(seq_len), weighted.reshape(seq_len, HEAD_DIM))]
    level_q, level_k, level_v = (head_queries, head_keys, head_values)
    for level_index in range(1, level_total):
        level_q, level_k, level_v = (halve_rows(level_q), halve_rows(level_k), halve_rows(level_v))
        level_rows = seq_len >> level_index
        pair_count = level_rows // (2 * BLOCK)
        block_queries = level_q.reshape(pair_count * 2, BLOCK, HEAD_DIM)
        partner_keys = level_k.reshape(pair_count, 2, BLOCK, HEAD_DIM)[:, ::-1].reshape(pair_count * 2, BLOCK, HEAD_DIM)
        partner_values = level_v.reshape(pair_count, 2, BLOCK, HEAD_DIM)[:, ::-1].reshape(pair_count * 2, BLOCK, HEAD_DIM)
        maxima, totals, weighted = attend(block_queries, partner_keys, partner_values)
        results.append((maxima.reshape(level_rows), totals.reshape(level_rows), weighted.reshape(level_rows, HEAD_DIM)))
    expanded = []
    for level_index in range(level_total):
        maxima, totals, weighted = results[level_index]
        factor = 2 ** level_index
        expanded.append((jnp.repeat(maxima, factor, axis=0), jnp.repeat(totals, factor, axis=0), jnp.repeat(weighted, factor, axis=0), float(factor)))
    overall = expanded[0][0]
    for entry in expanded[1:]:
        overall = jnp.maximum(overall, entry[0])
    norm_sum = jnp.zeros((seq_len,), jnp.float32)
    value_sum = jnp.zeros((seq_len, HEAD_DIM), jnp.float32)
    for maxima, totals, weighted, factor in expanded:
        scaled = factor * jnp.exp(maxima - overall)
        norm_sum = norm_sum + scaled * totals
        value_sum = value_sum + scaled[:, None] * weighted
    return value_sum / norm_sum[:, None]

def reference(queries, keys, values, gain):
    by_head_q = queries.reshape(TOKENS, HEADS, HEAD_DIM).transpose(1, 0, 2)
    by_head_k = keys.reshape(TOKENS, HEADS, HEAD_DIM).transpose(1, 0, 2)
    by_head_v = values.reshape(TOKENS, HEADS, HEAD_DIM).transpose(1, 0, 2)
    attended = lax.map(head_layer, (by_head_q, by_head_k, by_head_v))
    squares = lax.optimization_barrier(jnp.sum(attended * attended, axis=(0, 2))) / (HEADS * HEAD_DIM)
    normed = attended * lax.rsqrt(squares + 1e-06)[None, :, None] * gain.reshape(HEADS, 1, HEAD_DIM)
    return normed.transpose(1, 0, 2).reshape(TOKENS, HEADS * HEAD_DIM).astype(jnp.bfloat16)
```

```python
import functools
import math

import jax
import jax.numpy as jnp
from jax import lax
from jax.experimental import pallas as pl
from jax.experimental.pallas import tpu as pltpu
from jax.sharding import PartitionSpec as P

HEAD_DIM = 128
BLOCK = 128
GROUP = 256
LOG2_SCALE = math.log2(math.e) / math.sqrt(HEAD_DIM)
F32 = jnp.float32
BF16 = jnp.bfloat16
NT = (((1,), (1,)), ((), ()))
MIB = 1 << 20


def iota2(shape, dim):
    return lax.broadcasted_iota(jnp.int32, shape, dim)


def averaging(levels, width):
    parts = []
    for level in levels:
        shape = (width >> level, width)
        hit = (iota2(shape, 1) >> level) == iota2(shape, 0)
        parts.append(jnp.where(hit, 2.0**-level, 0.0))
    return jnp.concatenate(parts, axis=0).astype(BF16)


def slab_order(rows, slabs):
    shape = (rows, rows)
    per = rows // slabs
    row = iota2(shape, 0)
    source = (row % per) * slabs + row // per
    return jnp.where(iota2(shape, 1) == source, 1.0, 0.0).astype(BF16)


def twice(array, per):
    count, width = array.shape[0] // per, array.shape[1]
    wide = jnp.broadcast_to(array.reshape(count, 1, per, width), (count, 2, per, width))
    return wide.reshape(2 * count * per, width)


def halve_slabs(array, per):
    count, width = array.shape[0] // (2 * per), array.shape[1]
    pairs = array.reshape(count, 2, per, width)
    return ((pairs[:, 0] + pairs[:, 1]) * 0.5).reshape(count * per, width)


def level_step(q, k, v, coarse, per):
    scores = lax.dot_general(q, k, NT, preferred_element_type=F32)
    peak = jnp.max(scores, axis=1, keepdims=True)
    if coarse is not None:
        coarse_peak, coarse_norm, coarse_value = coarse
        coarse_peak = twice(coarse_peak, per)
        peak = jnp.maximum(peak, coarse_peak)
    weights = jnp.exp2((scores - peak) * LOG2_SCALE)
    norm = jnp.sum(weights, axis=1, keepdims=True)
    value = jnp.dot(weights.astype(BF16), v, preferred_element_type=F32)
    if coarse is not None:
        scale = 2.0 * jnp.exp2((coarse_peak - peak) * LOG2_SCALE)
        norm = norm + scale * twice(coarse_norm, per)
        value = value + scale * twice(coarse_value, per)
    return peak, norm, value


def pool_kernel(k_ref, v_ref, k1, v1, k2, v2, k3, v3, kv4, kv5, kv6, kv7, kv8, mat, mat2):
    step = pl.program_id(0)

    @pl.when(step == 0)
    def _():
        mat[...] = jnp.concatenate([averaging((1, 2, 3, 4), GROUP), jnp.zeros((16, GROUP), BF16)], axis=0)
        mat2[...] = jnp.concatenate([averaging((1, 2, 3, 4), BLOCK), jnp.zeros((8, BLOCK), BF16)], axis=0)

    for index, (ref, o1, o2, o3) in enumerate(((k_ref, k1, k2, k3), (v_ref, v1, v2, v3))):
        pooled = jnp.dot(mat[...], ref[...], preferred_element_type=F32).astype(BF16)
        o1[...] = pooled[:128]
        o2[...] = pooled[128:192]
        o3[...] = pooled[192:224]
        kv4[index, pl.ds(pl.multiple_of(step * 16, 16), 16), :] = pooled[224:240]

    @pl.when(step == pl.num_programs(0) - 1)
    def _():
        for index in range(2):
            pooled = jnp.dot(mat2[...], kv4[index], preferred_element_type=F32).astype(BF16)
            kv5[index] = pooled[:64]
            kv6[index] = pooled[64:96]
            kv7[index] = pooled[96:112]
            kv8[index] = pooled[112:128]


def pool(keys, values):
    rows, width = keys.shape
    groups = rows // GROUP
    shapes = []
    specs = []
    for level in (1, 2, 3):
        for _ in range(2):
            shapes.append(jax.ShapeDtypeStruct((rows >> level, width), BF16))
            specs.append(pl.BlockSpec((GROUP >> level, width), lambda g: (g, 0)))
    for count in (128, 64, 32, 16, 16):
        shapes.append(jax.ShapeDtypeStruct((2, count, width), BF16))
        specs.append(pl.BlockSpec((2, count, width), lambda g: (0, 0, 0)))
    block = pl.BlockSpec((GROUP, width), lambda g: (g, 0))
    return pl.pallas_call(
        pool_kernel,
        grid=(groups,),
        in_specs=[block, block],
        out_specs=specs,
        out_shape=shapes,
        scratch_shapes=[pltpu.VMEM((GROUP, GROUP), BF16), pltpu.VMEM((BLOCK, BLOCK), BF16)],
        compiler_params=pltpu.CompilerParams(vmem_limit_bytes=32 * MIB),
        cost_estimate=pl.CostEstimate(flops=2 * 2 * rows * GROUP * width, bytes_accessed=15 * MIB, transcendentals=0),
        name="pool",
    )(keys, values)


def near_kernel(q_ref, k0, v0, k1, v1, k2, v2, k3, v3, *rest):
    att_ref, log_ref, q4_ref, perm = rest[-4:]

    @pl.when(pl.program_id(0) == 0)
    def _():
        perm[...] = slab_order(GROUP, 16)

    heads = q_ref.shape[1] // HEAD_DIM
    lane = iota2((GROUP, HEAD_DIM), 1)
    logs = jnp.zeros((GROUP, HEAD_DIM), F32)
    for head in range(heads):
        cols = slice(head * HEAD_DIM, (head + 1) * HEAD_DIM)
        level = jnp.dot(perm[...], q_ref[:, cols], preferred_element_type=F32)
        queries = [level.astype(BF16)]
        for _ in range(4):
            level = halve_slabs(level, 16).astype(BF16)
            queries.append(level)
            level = level.astype(F32)
        q4_ref[:, cols] = queries[4]
        state = None
        for q, k, v in ((queries[3], k3, v3), (queries[2], k2, v2), (queries[1], k1, v1), (queries[0], k0, v0)):
            state = level_step(q, k[:, cols], v[:, cols], state, 16)
        peak, norm, value = state
        att_ref[:, cols] = (value * (1.0 / norm)).astype(BF16)
        logs = jnp.where(lane == head, peak * LOG2_SCALE + jnp.log2(norm), logs)
    log_ref[...] = logs


def near(queries, keys, values, pooled, start, count, previous):
    rows, width = queries.shape
    own = pl.BlockSpec((GROUP, width), lambda g: (start + g, 0))
    specs = [own, own, own]
    for level in (1, 2, 3):
        spec = pl.BlockSpec((BLOCK, width), lambda g, s=level - 1: (((start + g) >> s) ^ 1, 0))
        specs += [spec, spec]
    aliases = {}
    if previous is not None:
        aliases = {9: 0, 10: 1, 11: 2}
        specs += [pl.BlockSpec(memory_space=pl.ANY)] * 3
    return pl.pallas_call(
        near_kernel,
        grid=(count,),
        in_specs=specs,
        out_specs=[
            own,
            pl.BlockSpec((GROUP, HEAD_DIM), lambda g: (start + g, 0)),
            pl.BlockSpec((16, width), lambda g: (start + g, 0)),
        ],
        out_shape=[
            jax.ShapeDtypeStruct((rows, width), BF16),
            jax.ShapeDtypeStruct((rows, HEAD_DIM), F32),
            jax.ShapeDtypeStruct((rows >> 4, width), BF16),
        ],
        scratch_shapes=[pltpu.VMEM((GROUP, GROUP), BF16)],
        input_output_aliases=aliases,
        compiler_params=pltpu.CompilerParams(vmem_limit_bytes=40 * MIB),
        cost_estimate=pl.CostEstimate(
            flops=count * 8 * 2 * 2 * GROUP * GROUP * 256, bytes_accessed=count * 3 * MIB, transcendentals=count * 8 * 98304
        ),
        name="near",
    )(queries, keys, values, *pooled, *(previous or ()))


def far_kernel(
    q4_ref, s4, x_own, y2_own, y4_own, y6_own, x_far, y2_far, y4_far, y6_far, near_ref, log_ref,
    att_ref, sq_ref, coarse, coarse_log,
):
    step = pl.program_id(0)
    heads = near_ref.shape[1] // HEAD_DIM

    @pl.when(step == 0)
    def _():
        lane = iota2((BLOCK, HEAD_DIM), 1)
        logs = jnp.zeros((BLOCK, HEAD_DIM), F32)
        perm = slab_order(BLOCK, 16)
        for head in range(heads):
            cols = slice(head * HEAD_DIM, (head + 1) * HEAD_DIM)
            level = jnp.dot(perm, q4_ref[:, cols], preferred_element_type=F32)
            queries = [level.astype(BF16)]
            for _ in range(4):
                level = halve_slabs(level, 8).astype(BF16)
                queries.append(level)
                level = level.astype(F32)

            def rows(parts, part):
                return jnp.concatenate([ref[part, lo:hi, cols] for ref, lo, hi in parts], axis=0)

            sides = ((x_own, y2_own, y4_own, y6_own), (x_far, y2_far, y4_far, y6_far))
            level8 = [(r, lo, hi) for x, y2, y4, y6 in sides
                      for r, lo, hi in ((x, 16, 32), (y2, 80, 96), (y4, 48, 64), (y6, 48, 64))]
            level7 = [(r, lo, hi) for x, y2, y4, y6 in sides
                      for r, lo, hi in ((x, 0, 16), (y2, 64, 80), (y4, 32, 48), (y6, 32, 48))]
            level6 = [(r, 0, 32) for x, y2, y4, y6 in sides for r in (y4, y6)]
            level5 = [(y2, 0, 64) for x, y2, y4, y6 in sides]
            state = None
            for q, parts in zip(reversed(queries), (level8, level7, level6, level5, [(s4, 0, 128)])):
                state = level_step(q, rows(parts, 0), rows(parts, 1), state, 8)
            peak, norm, value = state
            value = value * (1.0 / norm)
            for slab in range(16):
                coarse[head, pl.ds(slab, 8, stride=16), :] = value[slab * 8 : slab * 8 + 8]
            logs = jnp.where(lane == head, peak * LOG2_SCALE + jnp.log2(norm) + 4.0, logs)
        for slab in range(16):
            coarse_log[pl.ds(slab, 8, stride=16), :] = logs[slab * 8 : slab * 8 + 8]

    here = pl.ds(pl.multiple_of(step * 16, 16), 16)
    gap = log_ref[...].reshape(16, 16, HEAD_DIM) - coarse_log[here, :][None]
    share = 1.0 / (1.0 + jnp.exp2(gap)).reshape(GROUP, HEAD_DIM)
    squares = jnp.zeros((GROUP, HEAD_DIM), F32)
    for head in range(heads):
        cols = slice(head * HEAD_DIM, (head + 1) * HEAD_DIM)
        part = near_ref[:, cols].astype(F32)
        delta = (coarse[head, here, :][None] - part.reshape(16, 16, HEAD_DIM)).reshape(GROUP, HEAD_DIM)
        attended = part + share[:, head : head + 1] * delta
        squares = squares + attended * attended
        att_ref[:, cols] = attended.astype(BF16)
    sums = lax.dot_general(
        jnp.ones((8, HEAD_DIM), F32), squares, NT, precision=lax.Precision.HIGHEST, preferred_element_type=F32
    )
    sq_ref[pl.ds(step, 1), :] = sums[:1]


def far(q4, s4, own, other, near_att, near_log):
    rows, width = near_att.shape
    groups = rows // GROUP
    whole = [pl.BlockSpec(a.shape, lambda g, n=a.ndim: (0,) * n) for a in (q4, s4, *own, *other)]
    block = pl.BlockSpec((GROUP, width), lambda g: (g, 0))
    return pl.pallas_call(
        far_kernel,
        grid=(groups,),
        in_specs=whole + [block, pl.BlockSpec((GROUP, HEAD_DIM), lambda g: (g, 0))],
        out_specs=[block, pl.BlockSpec((groups, GROUP), lambda g: (0, 0))],
        out_shape=[jax.ShapeDtypeStruct((rows, width), BF16), jax.ShapeDtypeStruct((groups, GROUP), F32)],
        scratch_shapes=[pltpu.VMEM((width // HEAD_DIM, BLOCK, HEAD_DIM), F32), pltpu.VMEM((BLOCK, HEAD_DIM), F32)],
        compiler_params=pltpu.CompilerParams(vmem_limit_bytes=40 * MIB),
        name="far",
    )(q4, s4, *own, *other, near_att, near_log)


def norm_kernel(features, att_ref, s0, s1, s2, s3, gain_ref, out_ref, perm):
    step = pl.program_id(0)

    @pl.when(step == 0)
    def _():
        shape = (GROUP, GROUP)
        source = (iota2(shape, 0) % 16) * 16 + iota2(shape, 0) // 16
        perm[...] = jnp.where(iota2(shape, 1) == source, 1.0, 0.0)

    here = pl.ds(step, 1)
    total = (s0[here, :] + s1[here, :]) + (s2[here, :] + s3[here, :])
    scale = lax.rsqrt(total / features + 1e-06)
    matrix = (perm[...] * scale).astype(BF16)
    mixed = jnp.dot(matrix, att_ref[...], preferred_element_type=F32)
    out_ref[...] = (mixed * gain_ref[...]).astype(BF16)


def normed(att, sums, gain, features):
    rows, width = att.shape
    groups = rows // GROUP
    block = pl.BlockSpec((GROUP, width), lambda g: (g, 0))
    whole = pl.BlockSpec((groups, GROUP), lambda g: (0, 0))
    return pl.pallas_call(
        functools.partial(norm_kernel, features),
        grid=(groups,),
        in_specs=[block, whole, whole, whole, whole, pl.BlockSpec((1, width), lambda g: (0, 0))],
        out_specs=block,
        out_shape=jax.ShapeDtypeStruct((rows, width), BF16),
        scratch_shapes=[pltpu.VMEM((GROUP, GROUP), F32)],
        compiler_params=pltpu.CompilerParams(vmem_limit_bytes=32 * MIB),
        name="norm",
    )(att, *sums, gain.reshape(1, width))


def swapped(array, axis, bits):
    return lax.ppermute(array, axis, [(i, i ^ bits) for i in range(lax.axis_size(axis))])


def local(queries, keys, values, gain):
    *pooled, kv4, kv5, kv6, kv7, kv8 = pool(keys, values)
    rows8 = kv8[:, :8]
    x7 = swapped(kv7, "seq", 8)
    x8a = swapped(rows8, "seq", 16)
    x8b = swapped(rows8, "seq", 24)
    s4 = swapped(kv4, "seq", 1)
    first = near(queries, keys, values, pooled, 0, 2, None)
    x_own = jnp.concatenate([x7, x8a, x8b], axis=1)
    to2 = jnp.concatenate([kv5, x_own], axis=1)
    to46 = jnp.concatenate([kv6, x_own], axis=1)
    own = [x_own, swapped(to2, "seq", 2), swapped(to46, "seq", 4), swapped(to46, "seq", 6)]
    second = near(queries, keys, values, pooled, 2, 4, first)
    other = [swapped(a, "seq", 1) for a in own]
    near_att, near_log, q4 = near(queries, keys, values, pooled, 6, 2, second)
    att, squares = far(q4, s4, own, other, near_att, near_log)
    sums = [squares] + [
        lax.ppermute(squares, "head", [(i, (i + s) % 4) for i in range(4)]) for s in (1, 2, 3)
    ]
    return normed(att, sums, gain, lax.axis_size("head") * queries.shape[1])


def solution(mesh):
    return jax.shard_map(
        local,
        mesh=mesh,
        in_specs=(P("seq", "head"), P("seq", "head"), P("seq", "head"), P("head")),
        out_specs=P("seq", "head"),
        check_vma=False,
    )
```

```python
import functools
import math

import jax
import jax.numpy as jnp
from jax import lax
from jax.experimental import pallas as pl
from jax.experimental.pallas import tpu as pltpu
from jax.sharding import PartitionSpec as P

HEAD_DIM = 128
BLOCK = 128
GROUP = 256
LOG2_SCALE = math.log2(math.e) / math.sqrt(HEAD_DIM)
F32 = jnp.float32
BF16 = jnp.bfloat16
NT = (((1,), (1,)), ((), ()))
MIB = 1 << 20


def iota2(shape, dim):
    return lax.broadcasted_iota(jnp.int32, shape, dim)


def averaging(levels, width):
    parts = []
    for level in levels:
        shape = (width >> level, width)
        hit = (iota2(shape, 1) >> level) == iota2(shape, 0)
        parts.append(jnp.where(hit, 2.0**-level, 0.0))
    return jnp.concatenate(parts, axis=0).astype(BF16)


def slab_order(rows, slabs):
    shape = (rows, rows)
    per = rows // slabs
    row = iota2(shape, 0)
    source = (row % per) * slabs + row // per
    return jnp.where(iota2(shape, 1) == source, 1.0, 0.0).astype(BF16)


def twice(array, per):
    count, width = array.shape[0] // per, array.shape[1]
    wide = jnp.broadcast_to(array.reshape(count, 1, per, width), (count, 2, per, width))
    return wide.reshape(2 * count * per, width)


def halve_slabs(array, per):
    count, width = array.shape[0] // (2 * per), array.shape[1]
    pairs = array.reshape(count, 2, per, width)
    return ((pairs[:, 0] + pairs[:, 1]) * 0.5).reshape(count * per, width)


def score_all(queries, keys):
    return [lax.dot_general(q, k, NT, preferred_element_type=F32) for q, k in zip(queries, keys)]


def weigh_all(scores, per):
    results, peak = [], None
    for index, level in enumerate(scores):
        own, scale = jnp.max(level, axis=1, keepdims=True), None
        if peak is not None:
            coarse = twice(peak, per)
            own = jnp.maximum(own, coarse)
            scale = 2.0 * jnp.exp2((coarse - own) * LOG2_SCALE)
        peak = own
        weights = jnp.exp2((level - peak) * LOG2_SCALE)
        norm = None if index + 1 == len(scores) else jnp.sum(weights, axis=1, keepdims=True)
        results.append((weights.astype(BF16), norm, scale))
    return results, peak


def sum_all(results, values, per):
    norm = value = None
    for index, ((weights, total, scale), v) in enumerate(zip(results, values)):
        if total is None:
            v = jnp.concatenate([v, jnp.ones_like(v)], axis=1)
        summed = jnp.dot(weights, v, preferred_element_type=F32)
        if total is None:
            summed, total = summed[:, :HEAD_DIM], summed[:, HEAD_DIM:]
        if scale is not None:
            total = total + scale * twice(norm, per)
            summed = summed + scale * twice(value, per)
        norm, value = total, summed
    return norm, value


def pool_kernel(
    k_hbm, v_hbm, k0, v0, k1, v1, k2, v2, k3, v3, kv4, kv5, kv6, kv7, kv8, sems
):
    groups = k0.shape[0] // GROUP
    sides = ((k_hbm, k0, k1, k2, k3), (v_hbm, v0, v1, v2, v3))

    def copy(index, group):
        rows = pl.ds(group * GROUP, GROUP)
        return pltpu.make_async_copy(sides[index][0].at[rows], sides[index][1].at[rows], sems.at[index, group])

    for group in range(groups):
        for index in range(2):
            copy(index, group).start()
    matrix = jnp.concatenate([averaging((1, 2, 3, 4), GROUP), jnp.zeros((16, GROUP), BF16)], axis=0)
    for group in range(groups):
        for index, (_, o0, o1, o2, o3) in enumerate(sides):
            copy(index, group).wait()
            rows = o0[group * GROUP : (group + 1) * GROUP]
            pooled = jnp.dot(matrix, rows, preferred_element_type=F32).astype(BF16)
            o1[group * 128 : group * 128 + 128] = pooled[:128]
            o2[group * 64 : group * 64 + 64] = pooled[128:192]
            o3[group * 32 : group * 32 + 32] = pooled[192:224]
            kv4[index, group * 16 : group * 16 + 16] = pooled[224:240]
    matrix = jnp.concatenate([averaging((1, 2, 3, 4), BLOCK), jnp.zeros((8, BLOCK), BF16)], axis=0)
    for index in range(2):
        pooled = jnp.dot(matrix, kv4[index], preferred_element_type=F32).astype(BF16)
        kv5[index] = pooled[:64]
        kv6[index] = pooled[64:96]
        kv7[index] = pooled[96:112]
        kv8[index] = pooled[112:128]


def pool(keys, values):
    rows, width = keys.shape
    shapes = [pltpu.VMEM((rows >> level, width), BF16) for level in range(4) for _ in range(2)]
    shapes += [jax.ShapeDtypeStruct((2, count, width), BF16) for count in (128, 64, 32, 16, 16)]
    return pl.pallas_call(
        pool_kernel,
        in_specs=[pl.BlockSpec(memory_space=pl.ANY)] * 2,
        out_specs=[pl.BlockSpec(memory_space=pltpu.VMEM)] * len(shapes),
        out_shape=shapes,
        scratch_shapes=[pltpu.SemaphoreType.DMA((2, rows // GROUP))],
        compiler_params=pltpu.CompilerParams(vmem_limit_bytes=28 * MIB),
        cost_estimate=pl.CostEstimate(flops=2 * 2 * rows * GROUP * width, bytes_accessed=8 * MIB, transcendentals=0),
        name="pool",
    )(pltpu.with_memory_space_constraint(keys, pltpu.HBM), pltpu.with_memory_space_constraint(values, pltpu.HBM))


def near_kernel(start, q_ref, k0, v0, k1, v1, k2, v2, k3, v3, att_ref, log_ref, q4_ref):
    perm = slab_order(GROUP, 16)
    heads = [slice(c, c + HEAD_DIM) for c in range(0, q_ref.shape[1], HEAD_DIM)]
    lane = iota2((GROUP, HEAD_DIM), 1)

    def at(index, count):
        return pl.ds(pl.multiple_of(index * count, count), count)

    @pl.loop(0, att_ref.shape[0] // GROUP)
    def _(step):
        group = start + step
        level = jnp.dot(perm, q_ref[at(group, GROUP), :], preferred_element_type=F32)
        queries = [level.astype(BF16)]
        for _ in range(4):
            queries.insert(0, halve_slabs(level, 16).astype(BF16))
            level = queries[0].astype(F32)
        q4_ref[at(step, 16), :] = queries.pop(0)
        places = [at((group >> level) ^ 1, BLOCK) for level in (2, 1, 0)] + [at(group, GROUP)]
        keys, values = (
            [[ref[place, cols] for ref, place in zip(refs, places)] for cols in heads]
            for refs in ((k3, k2, k1, k0), (v3, v2, v1, v0))
        )
        scores = [score_all([q[:, cols] for q in queries], keys[head]) for head, cols in enumerate(heads)]
        weighed = [weigh_all(levels, 16) for levels in scores]
        logs = jnp.zeros((GROUP, HEAD_DIM), F32)
        for head, cols in enumerate(heads):
            results, peak = weighed[head]
            norm, value = sum_all(results, values[head], 16)
            att_ref[at(step, GROUP), cols] = (value * (1.0 / norm)).astype(BF16)
            logs = jnp.where(lane == head, peak * LOG2_SCALE + jnp.log2(norm), logs)
        log_ref[at(step, GROUP), :] = logs


def near(queries, pooled, start, count):
    width = queries.shape[1]
    return pl.pallas_call(
        functools.partial(near_kernel, start),
        in_specs=[pl.BlockSpec(memory_space=pltpu.VMEM)] * 9,
        out_specs=[pl.BlockSpec(memory_space=pltpu.VMEM)] * 3,
        out_shape=[
            pltpu.VMEM((count * GROUP, width), BF16),
            pltpu.VMEM((count * GROUP, HEAD_DIM), F32),
            pltpu.VMEM((count * 16, width), BF16),
        ],
        compiler_params=pltpu.CompilerParams(vmem_limit_bytes=28 * MIB),
        cost_estimate=pl.CostEstimate(
            flops=count * 8 * 2 * 2 * GROUP * GROUP * 256, bytes_accessed=count * 3 * MIB, transcendentals=count * 8 * 98304
        ),
        name="near",
    )(queries, *pooled)


def far_kernel(s4, x_own, y2_own, y4_own, y6_own, x_far, y2_far, y4_far, y6_far, *rest):
    parts, (att_ref, sq_ref, coarse, coarse_log) = rest[:-4], rest[-4:]
    near_refs, log_refs, q4_refs = parts[0::3], parts[1::3], parts[2::3]
    heads = [slice(c, c + HEAD_DIM) for c in range(0, att_ref.shape[1], HEAD_DIM)]

    def coarse_levels():
        q4 = jnp.concatenate([ref[...] for ref in q4_refs], axis=0)
        level = jnp.dot(slab_order(BLOCK, 16), q4, preferred_element_type=F32)
        queries = [level.astype(BF16)]
        for _ in range(4):
            queries.insert(0, halve_slabs(level, 8).astype(BF16))
            level = queries[0].astype(F32)
        sides = ((x_own, y2_own, y4_own, y6_own), (x_far, y2_far, y4_far, y6_far))
        pieces = [[], [], [], [], [(s4, 0, 128)]]
        for x, y2, y4, y6 in sides:
            pieces[0] += [(x, 16, 32), (y2, 80, 96), (y4, 48, 64), (y6, 48, 64)]
            pieces[1] += [(x, 0, 16), (y2, 64, 80), (y4, 32, 48), (y6, 32, 48)]
            pieces[2] += [(y4, 0, 32), (y6, 0, 32)]
            pieces[3] += [(y2, 0, 64)]
        keys, values = (
            [jnp.concatenate([ref[part, lo:hi, :] for ref, lo, hi in level], axis=0) for level in pieces]
            for part in (0, 1)
        )
        scores = [score_all([q[:, cols] for q in queries], [k[:, cols] for k in keys]) for cols in heads]
        weighed = [weigh_all(levels, 8) for levels in scores]
        lane = iota2((BLOCK, HEAD_DIM), 1)
        logs = jnp.zeros((BLOCK, HEAD_DIM), F32)
        for head, cols in enumerate(heads):
            results, peak = weighed[head]
            norm, value = sum_all(results, [v[:, cols] for v in values], 8)
            value = value * (1.0 / norm)
            for slab in range(16):
                coarse[head, pl.ds(slab, 8, stride=16), :] = value[slab * 8 : slab * 8 + 8]
            logs = jnp.where(lane == head, peak * LOG2_SCALE + jnp.log2(norm) + 4.0, logs)
        for slab in range(16):
            coarse_log[pl.ds(slab, 8, stride=16), :] = logs[slab * 8 : slab * 8 + 8]

    def merge(near_ref, log_ref, first, step):
        def at(index, count):
            return pl.ds(pl.multiple_of(index * count, count), count)

        group = first + step
        gap = log_ref[at(step, GROUP), :].reshape(16, 16, HEAD_DIM) - coarse_log[at(group, 16), :][None]
        share = (1.0 / (1.0 + jnp.exp2(gap))).reshape(GROUP, HEAD_DIM)
        squares = jnp.zeros((GROUP, HEAD_DIM), F32)
        for head, cols in enumerate(heads):
            part = near_ref[at(step, GROUP), cols].astype(F32)
            delta = (coarse[head, at(group, 16), :][None] - part.reshape(16, 16, HEAD_DIM)).reshape(GROUP, HEAD_DIM)
            attended = part + share[:, head : head + 1] * delta
            squares = squares + attended * attended
            att_ref[at(group, GROUP), cols] = attended.astype(BF16)
        sums = lax.dot_general(
            jnp.ones((8, HEAD_DIM), F32), squares, NT, precision=lax.Precision.HIGHEST, preferred_element_type=F32
        )
        sq_ref[pl.ds(group, 1), :] = sums[:1]

    coarse_levels()
    first = 0
    for near_ref, log_ref in zip(near_refs, log_refs):
        count = near_ref.shape[0] // GROUP

        @pl.loop(0, count)
        def _(step, near_ref=near_ref, log_ref=log_ref, first=first):
            merge(near_ref, log_ref, first, step)

        first += count


def far(s4, own, other, parts):
    operands = [s4, *own, *other, *[array for part in parts for array in part]]
    rows, width = sum(part[0].shape[0] for part in parts), s4.shape[2]
    whole = pl.BlockSpec(memory_space=pltpu.VMEM)
    return pl.pallas_call(
        far_kernel,
        in_specs=[whole] * len(operands),
        out_specs=[whole, whole],
        out_shape=[pltpu.VMEM((rows, width), BF16), jax.ShapeDtypeStruct((rows // GROUP, GROUP), F32)],
        scratch_shapes=[pltpu.VMEM((width // HEAD_DIM, BLOCK, HEAD_DIM), F32), pltpu.VMEM((BLOCK, HEAD_DIM), F32)],
        compiler_params=pltpu.CompilerParams(vmem_limit_bytes=28 * MIB),
        name="far",
    )(*operands)


def norm_kernel(features, att_ref, s0, s1, s2, s3, gain_ref, out_hbm, out_vmem, sems):
    shape = (GROUP, GROUP)
    source = (iota2(shape, 0) % 16) * 16 + iota2(shape, 0) // 16
    hit = iota2(shape, 1) == source
    scale = lax.rsqrt(((s0[...] + s1[...]) + (s2[...] + s3[...])) / features + 1e-06)
    copies = []
    for group in range(att_ref.shape[0] // GROUP):
        rows = pl.ds(group * GROUP, GROUP)
        matrix = jnp.where(hit, scale[group : group + 1], 0.0).astype(BF16)
        mixed = jnp.dot(matrix, att_ref[rows, :], preferred_element_type=F32)
        out_vmem[rows, :] = (mixed * gain_ref[...]).astype(BF16)
        copies.append(pltpu.make_async_copy(out_vmem.at[rows], out_hbm.at[rows], sems.at[group]))
        copies[-1].start()
    for copy in copies:
        copy.wait()


def normed(att, sums, gain, features):
    rows, width = att.shape
    whole = pl.BlockSpec(memory_space=pltpu.VMEM)
    return pl.pallas_call(
        functools.partial(norm_kernel, features),
        in_specs=[whole] * 6,
        out_specs=pl.BlockSpec(memory_space=pl.ANY),
        out_shape=jax.ShapeDtypeStruct((rows, width), BF16),
        scratch_shapes=[pltpu.VMEM((rows, width), BF16), pltpu.SemaphoreType.DMA((rows // GROUP,))],
        compiler_params=pltpu.CompilerParams(vmem_limit_bytes=28 * MIB),
        name="norm",
    )(att, *sums, gain.reshape(1, width))


def swapped(array, axis, bits):
    return lax.ppermute(array, axis, [(i, i ^ bits) for i in range(lax.axis_size(axis))])


def local(queries, keys, values, gain):
    *pooled, kv4, kv5, kv6, kv7, kv8 = pool(keys, values)
    rows8 = kv8[:, :8]
    x7 = swapped(kv7, "seq", 8)
    x8a = swapped(rows8, "seq", 16)
    x8b = swapped(rows8, "seq", 24)
    s4 = swapped(kv4, "seq", 1)
    first = near(queries, pooled, 0, 2)
    x7, x8a, x8b, first = lax.optimization_barrier((x7, x8a, x8b, first))
    x_own = jnp.concatenate([x7, x8a, x8b], axis=1)
    to2 = jnp.concatenate([kv5, x_own], axis=1)
    to46 = jnp.concatenate([kv6, x_own], axis=1)
    own = [x_own, swapped(to2, "seq", 2), swapped(to46, "seq", 4), swapped(to46, "seq", 6)]
    second = near(queries, pooled, 2, 4)
    own, second = lax.optimization_barrier((own, second))
    other = [swapped(a, "seq", 1) for a in own]
    third = near(queries, pooled, 6, 2)
    att, squares = far(s4, own, other, (first, second, third))
    sums = [squares] + [
        lax.ppermute(squares, "head", [(i, (i + s) % 4) for i in range(4)]) for s in (1, 2, 3)
    ]
    return normed(att, sums, gain, lax.axis_size("head") * queries.shape[1])


def solution(mesh):
    return jax.shard_map(
        local,
        mesh=mesh,
        in_specs=(P("seq", "head"), P("seq", "head"), P("seq", "head"), P("head")),
        out_specs=P("seq", "head"),
        check_vma=False,
    )
```

```python
import functools
import math

import jax
import jax.numpy as jnp
from jax import lax
from jax.experimental import pallas as pl
from jax.experimental.pallas import tpu as pltpu
from jax.sharding import PartitionSpec as P

HEAD_DIM = 128
BLOCK = 128
GROUP = 256
LOG2_SCALE = math.log2(math.e) / math.sqrt(HEAD_DIM)
F32 = jnp.float32
BF16 = jnp.bfloat16
NT = (((1,), (1,)), ((), ()))
MIB = 1 << 20
SPLIT = (2, 5, 1)


def iota2(shape, dim):
    return lax.broadcasted_iota(jnp.int32, shape, dim)


def averaging(levels, width):
    parts = []
    for level in levels:
        shape = (width >> level, width)
        hit = (iota2(shape, 1) >> level) == iota2(shape, 0)
        parts.append(jnp.where(hit, 2.0**-level, 0.0))
    return jnp.concatenate(parts, axis=0).astype(BF16)


def slab_order(rows, slabs):
    shape = (rows, rows)
    per = rows // slabs
    row = iota2(shape, 0)
    source = (row % per) * slabs + row // per
    return jnp.where(iota2(shape, 1) == source, 1.0, 0.0).astype(BF16)


def twice(array, per):
    count, width = array.shape[0] // per, array.shape[1]
    wide = jnp.broadcast_to(array.reshape(count, 1, per, width), (count, 2, per, width))
    return wide.reshape(2 * count * per, width)


def halve_slabs(array, per):
    count, width = array.shape[0] // (2 * per), array.shape[1]
    pairs = array.reshape(count, 2, per, width)
    return ((pairs[:, 0] + pairs[:, 1]) * 0.5).reshape(count * per, width)


def score_all(queries, keys):
    return [lax.dot_general(q, k, NT, preferred_element_type=F32) for q, k in zip(queries, keys)]


def weigh_all(scores, per):
    results, peak = [], None
    for index, level in enumerate(scores):
        own, scale = jnp.max(level, axis=1, keepdims=True), None
        if peak is not None:
            coarse = twice(peak, per)
            own = jnp.maximum(own, coarse)
            scale = 2.0 * jnp.exp2((coarse - own) * LOG2_SCALE)
        peak = own
        weights = jnp.exp2((level - peak) * LOG2_SCALE)
        norm = None if index + 1 == len(scores) else jnp.sum(weights, axis=1, keepdims=True)
        results.append((weights.astype(BF16), norm, scale))
    return results, peak


def sum_all(results, values, per):
    norm = value = None
    for index, ((weights, total, scale), v) in enumerate(zip(results, values)):
        if total is None:
            v = jnp.concatenate([v, jnp.ones_like(v)], axis=1)
        summed = jnp.dot(weights, v, preferred_element_type=F32)
        if total is None:
            summed, total = summed[:, :HEAD_DIM], summed[:, HEAD_DIM:]
        if scale is not None:
            total = total + scale * twice(norm, per)
            summed = summed + scale * twice(value, per)
        norm, value = total, summed
    return norm, value


def pool_kernel(
    k_hbm, v_hbm, k0, v0, k1, v1, k2, v2, k3, v3, kv4, kv5, kv6, kv7, kv8, sems
):
    groups = k0.shape[0] // GROUP
    sides = ((k_hbm, k0, k1, k2, k3), (v_hbm, v0, v1, v2, v3))

    def copy(index, group):
        rows = pl.ds(group * GROUP, GROUP)
        return pltpu.make_async_copy(sides[index][0].at[rows], sides[index][1].at[rows], sems.at[index, group])

    ahead = 3
    for group in range(ahead):
        for index in range(2):
            copy(index, group).start()
    matrix = jnp.concatenate([averaging((1, 2, 3, 4), GROUP), jnp.zeros((16, GROUP), BF16)], axis=0)
    for group in range(groups):
        for index, (_, o0, o1, o2, o3) in enumerate(sides):
            copy(index, group).wait()
            if group + ahead < groups:
                copy(index, group + ahead).start()
            rows = o0[group * GROUP : (group + 1) * GROUP]
            pooled = jnp.dot(matrix, rows, preferred_element_type=F32).astype(BF16)
            o1[group * 128 : group * 128 + 128] = pooled[:128]
            o2[group * 64 : group * 64 + 64] = pooled[128:192]
            o3[group * 32 : group * 32 + 32] = pooled[192:224]
            kv4[index, group * 16 : group * 16 + 16] = pooled[224:240]
    matrix = jnp.concatenate([averaging((1, 2, 3, 4), BLOCK), jnp.zeros((8, BLOCK), BF16)], axis=0)
    for index in range(2):
        pooled = jnp.dot(matrix, kv4[index], preferred_element_type=F32).astype(BF16)
        kv5[index] = pooled[:64]
        kv6[index] = pooled[64:96]
        kv7[index] = pooled[96:112]
        kv8[index] = pooled[112:128]


def pool(keys, values):
    rows, width = keys.shape
    shapes = [pltpu.VMEM((rows >> level, width), BF16) for level in range(4) for _ in range(2)]
    shapes += [jax.ShapeDtypeStruct((2, count, width), BF16) for count in (128, 64, 32, 16, 16)]
    return pl.pallas_call(
        pool_kernel,
        in_specs=[pl.BlockSpec(memory_space=pl.ANY)] * 2,
        out_specs=[pl.BlockSpec(memory_space=pltpu.VMEM)] * len(shapes),
        out_shape=shapes,
        scratch_shapes=[pltpu.SemaphoreType.DMA((2, rows // GROUP))],
        compiler_params=pltpu.CompilerParams(vmem_limit_bytes=28 * MIB),
        cost_estimate=pl.CostEstimate(flops=2 * 2 * rows * GROUP * width, bytes_accessed=8 * MIB, transcendentals=0),
        name="pool",
    )(pltpu.with_memory_space_constraint(keys, pltpu.HBM), pltpu.with_memory_space_constraint(values, pltpu.HBM))


def near_kernel(start, q_ref, k0, v0, k1, v1, k2, v2, k3, v3, att_ref, log_ref, q4_ref):
    perm = slab_order(GROUP, 16)
    heads = [slice(c, c + HEAD_DIM) for c in range(0, q_ref.shape[1], HEAD_DIM)]
    lane = iota2((GROUP, HEAD_DIM), 1)

    def at(index, count):
        return pl.ds(pl.multiple_of(index * count, count), count)

    @pl.loop(0, att_ref.shape[0] // GROUP)
    def _(step):
        group = start + step
        level = jnp.dot(perm, q_ref[at(group, GROUP), :], preferred_element_type=F32)
        queries = [level.astype(BF16)]
        for _ in range(4):
            queries.insert(0, halve_slabs(level, 16).astype(BF16))
            level = queries[0].astype(F32)
        q4_ref[at(step, 16), :] = queries.pop(0)
        places = [at((group >> level) ^ 1, BLOCK) for level in (2, 1, 0)] + [at(group, GROUP)]
        keys, values = (
            [[ref[place, cols] for ref, place in zip(refs, places)] for cols in heads]
            for refs in ((k3, k2, k1, k0), (v3, v2, v1, v0))
        )
        scores = [score_all([q[:, cols] for q in queries], keys[head]) for head, cols in enumerate(heads)]
        weighed = [weigh_all(levels, 16) for levels in scores]
        logs = jnp.zeros((GROUP, HEAD_DIM), F32)
        for head, cols in enumerate(heads):
            results, peak = weighed[head]
            norm, value = sum_all(results, values[head], 16)
            att_ref[at(step, GROUP), cols] = (value * (1.0 / norm)).astype(BF16)
            logs = jnp.where(lane == head, peak * LOG2_SCALE + jnp.log2(norm), logs)
        log_ref[at(step, GROUP), :] = logs


def near(queries, pooled, start, count):
    width = queries.shape[1]
    return pl.pallas_call(
        functools.partial(near_kernel, start),
        in_specs=[pl.BlockSpec(memory_space=pltpu.VMEM)] * 9,
        out_specs=[pl.BlockSpec(memory_space=pltpu.VMEM)] * 3,
        out_shape=[
            pltpu.VMEM((count * GROUP, width), BF16),
            pltpu.VMEM((count * GROUP, HEAD_DIM), F32),
            pltpu.VMEM((count * 16, width), BF16),
        ],
        compiler_params=pltpu.CompilerParams(vmem_limit_bytes=28 * MIB),
        cost_estimate=pl.CostEstimate(
            flops=count * 8 * 2 * 2 * GROUP * GROUP * 256, bytes_accessed=count * 3 * MIB, transcendentals=count * 8 * 98304
        ),
        name="near",
    )(queries, *pooled)


def far_kernel(s4, *rest):
    sides, rest = (rest[:5], rest[5:10]), rest[10:]
    parts, (att_ref, sq_ref, coarse, coarse_log) = rest[:-4], rest[-4:]
    near_refs, log_refs, q4_refs = parts[0::3], parts[1::3], parts[2::3]
    heads = [slice(c, c + HEAD_DIM) for c in range(0, att_ref.shape[1], HEAD_DIM)]

    def coarse_levels():
        q4 = jnp.concatenate([ref[...] for ref in q4_refs], axis=0)
        level = jnp.dot(slab_order(BLOCK, 16), q4, preferred_element_type=F32)
        queries = [level.astype(BF16)]
        for _ in range(4):
            queries.insert(0, halve_slabs(level, 8).astype(BF16))
            level = queries[0].astype(F32)
        pieces = [[], [], [], [], [(s4, 0, 128)]]
        for l5, x_own, y2, y4, y6 in sides:
            along_x = [(x_own, 0), (y2, 0), (y4, 32), (y6, 32)]
            pieces[0] += [(ref, lo + 16, lo + 32) for ref, lo in along_x]
            pieces[1] += [(ref, lo, lo + 16) for ref, lo in along_x]
            pieces[2] += [(y4, 0, 32), (y6, 0, 32)]
            pieces[3] += [(l5, 0, 64)]
        keys, values = (
            [jnp.concatenate([ref[part, lo:hi, :] for ref, lo, hi in level], axis=0) for level in pieces]
            for part in (0, 1)
        )
        scores = [score_all([q[:, cols] for q in queries], [k[:, cols] for k in keys]) for cols in heads]
        weighed = [weigh_all(levels, 8) for levels in scores]
        lane = iota2((BLOCK, HEAD_DIM), 1)
        logs = jnp.zeros((BLOCK, HEAD_DIM), F32)
        for head, cols in enumerate(heads):
            results, peak = weighed[head]
            norm, value = sum_all(results, [v[:, cols] for v in values], 8)
            value = value * (1.0 / norm)
            for slab in range(16):
                coarse[head, pl.ds(slab, 8, stride=16), :] = value[slab * 8 : slab * 8 + 8]
            logs = jnp.where(lane == head, peak * LOG2_SCALE + jnp.log2(norm) + 4.0, logs)
        for slab in range(16):
            coarse_log[pl.ds(slab, 8, stride=16), :] = logs[slab * 8 : slab * 8 + 8]

    def merge(near_ref, log_ref, first, step):
        def at(index, count):
            return slice(index * count, (index + 1) * count)

        group = first + step
        gap = log_ref[at(step, GROUP), :].reshape(16, 16, HEAD_DIM) - coarse_log[at(group, 16), :][None]
        share = (1.0 / (1.0 + jnp.exp2(gap))).reshape(GROUP, HEAD_DIM)
        squares = jnp.zeros((GROUP, HEAD_DIM), F32)
        for head, cols in enumerate(heads):
            part = near_ref[at(step, GROUP), cols].astype(F32)
            delta = (coarse[head, at(group, 16), :][None] - part.reshape(16, 16, HEAD_DIM)).reshape(GROUP, HEAD_DIM)
            attended = part + share[:, head : head + 1] * delta
            squares = squares + attended * attended
            att_ref[at(group, GROUP), cols] = attended.astype(BF16)
        high = squares.astype(BF16)
        low = (squares - high.astype(F32)).astype(BF16)
        ones = jnp.ones((16, 2 * HEAD_DIM), BF16)
        pair = jnp.concatenate([high, low], axis=1)
        sums = lax.dot_general(ones, pair, NT, preferred_element_type=F32)
        sq_ref[group : group + 1] = sums[:1]

    coarse_levels()
    first = 0
    for near_ref, log_ref in zip(near_refs, log_refs):
        count = near_ref.shape[0] // GROUP
        for step in range(count):
            merge(near_ref, log_ref, first, step)
        first += count


def far(s4, own, other, parts):
    operands = [s4, *own, *other, *[array for part in parts for array in part]]
    rows, width = sum(part[0].shape[0] for part in parts), s4.shape[2]
    whole = pl.BlockSpec(memory_space=pltpu.VMEM)
    return pl.pallas_call(
        far_kernel,
        in_specs=[whole] * len(operands),
        out_specs=[whole, whole],
        out_shape=[pltpu.VMEM((rows, width), BF16), jax.ShapeDtypeStruct((rows // GROUP, GROUP), F32)],
        scratch_shapes=[pltpu.VMEM((width // HEAD_DIM, BLOCK, HEAD_DIM), F32), pltpu.VMEM((BLOCK, HEAD_DIM), F32)],
        compiler_params=pltpu.CompilerParams(vmem_limit_bytes=28 * MIB),
        name="far",
    )(*operands)


def norm_kernel(features, att_ref, s0, s1, s2, s3, gain_ref, out_hbm, out_vmem, sems):
    shape = (GROUP, GROUP)
    source = (iota2(shape, 0) % 16) * 16 + iota2(shape, 0) // 16
    hit = iota2(shape, 1) == source
    scale = lax.rsqrt(((s0[...] + s1[...]) + (s2[...] + s3[...])) / features + 1e-06)
    copies = []
    for group in range(att_ref.shape[0] // GROUP):
        rows = pl.ds(group * GROUP, GROUP)
        matrix = jnp.where(hit, scale[group : group + 1], 0.0).astype(BF16)
        mixed = jnp.dot(matrix, att_ref[rows, :], preferred_element_type=F32)
        out_vmem[rows, :] = (mixed * gain_ref[...]).astype(BF16)
        copies.append(pltpu.make_async_copy(out_vmem.at[rows], out_hbm.at[rows], sems.at[group]))
        copies[-1].start()
    for copy in copies:
        copy.wait()


def normed(att, sums, gain, features):
    rows, width = att.shape
    whole = pl.BlockSpec(memory_space=pltpu.VMEM)
    return pl.pallas_call(
        functools.partial(norm_kernel, features),
        in_specs=[whole] * 6,
        out_specs=pl.BlockSpec(memory_space=pl.ANY),
        out_shape=jax.ShapeDtypeStruct((rows, width), BF16),
        scratch_shapes=[pltpu.VMEM((rows, width), BF16), pltpu.SemaphoreType.DMA((rows // GROUP,))],
        compiler_params=pltpu.CompilerParams(vmem_limit_bytes=28 * MIB),
        name="norm",
    )(att, *sums, gain.reshape(1, width))


def swapped(array, axis, bits):
    return lax.ppermute(array, axis, [(i, i ^ bits) for i in range(lax.axis_size(axis))])


def local(queries, keys, values, gain):
    *pooled, kv4, kv5, kv6, kv7, kv8 = pool(keys, values)
    queries, kv7, kv8 = lax.optimization_barrier((queries, kv7, kv8))
    rows8 = kv8[:, :8]
    x7 = swapped(kv7, "seq", 8)
    x8a = swapped(rows8, "seq", 16)
    x8b = swapped(rows8, "seq", 24)
    l5 = swapped(kv5, "seq", 2)
    s4 = swapped(kv4, "seq", 1)
    first = near(queries, pooled, 0, SPLIT[0])
    x7, x8a, x8b, first = lax.optimization_barrier((x7, x8a, x8b, first))
    x_own = jnp.concatenate([x7, x8a, x8b], axis=1)
    both = jnp.concatenate([kv6, x_own], axis=1)
    early = [l5, x_own]
    own = [swapped(x_own, "seq", 2), swapped(both, "seq", 4), swapped(both, "seq", 6)]
    early_other = [swapped(a, "seq", 1) for a in early]
    second = near(queries, pooled, SPLIT[0], SPLIT[1])
    own, second = lax.optimization_barrier((own, second))
    other = [swapped(a, "seq", 1) for a in own]
    third = near(queries, pooled, SPLIT[0] + SPLIT[1], SPLIT[2])
    att, squares = far(s4, early + own, early_other + other, (first, second, third))
    sums = [squares] + [
        lax.ppermute(squares, "head", [(i, (i + s) % 4) for i in range(4)]) for s in (1, 2, 3)
    ]
    return normed(att, sums, gain, lax.axis_size("head") * queries.shape[1])


def solution(mesh):
    return jax.shard_map(
        local,
        mesh=mesh,
        in_specs=(P("seq", "head"), P("seq", "head"), P("seq", "head"), P("head")),
        out_specs=P("seq", "head"),
        check_vma=False,
    )
```

```python
import functools
import math

import jax
import jax.numpy as jnp
from jax import lax
from jax.experimental import pallas as pl
from jax.experimental.pallas import tpu as pltpu
from jax.sharding import PartitionSpec as P

HEAD_DIM = 128
BLOCK = 128
GROUP = 256
LOG2_SCALE = math.log2(math.e) / math.sqrt(HEAD_DIM)
F32 = jnp.float32
BF16 = jnp.bfloat16
NT = (((1,), (1,)), ((), ()))
MIB = 1 << 20
SPLIT = (2, 5, 1)
TOGETHER = 2


def iota2(shape, dim):
    return lax.broadcasted_iota(jnp.int32, shape, dim)


def averaging(levels, width):
    parts = []
    for level in levels:
        shape = (width >> level, width)
        hit = (iota2(shape, 1) >> level) == iota2(shape, 0)
        parts.append(jnp.where(hit, 2.0**-level, 0.0))
    return jnp.concatenate(parts, axis=0).astype(BF16)


def slab_order(rows, slabs):
    shape = (rows, rows)
    per = rows // slabs
    row = iota2(shape, 0)
    source = (row % per) * slabs + row // per
    return jnp.where(iota2(shape, 1) == source, 1.0, 0.0).astype(BF16)


def twice(array, per):
    count, width = array.shape[0] // per, array.shape[1]
    wide = jnp.broadcast_to(array.reshape(count, 1, per, width), (count, 2, per, width))
    return wide.reshape(2 * count * per, width)


def halve_slabs(array, per):
    count, width = array.shape[0] // (2 * per), array.shape[1]
    pairs = array.reshape(count, 2, per, width)
    return ((pairs[:, 0] + pairs[:, 1]) * 0.5).reshape(count * per, width)


def score_all(queries, keys):
    return [lax.dot_general(q, k, NT, preferred_element_type=F32) for q, k in zip(queries, keys)]


def weigh_all(scores, per):
    results, peak = [], None
    for index, level in enumerate(scores):
        own, scale = jnp.max(level, axis=1, keepdims=True), None
        if peak is not None:
            coarse = twice(peak, per)
            own = jnp.maximum(own, coarse)
            scale = 2.0 * jnp.exp2((coarse - own) * LOG2_SCALE)
        peak = own
        weights = jnp.exp2((level - peak) * LOG2_SCALE)
        norm = None if index + 1 == len(scores) else jnp.sum(weights, axis=1, keepdims=True)
        results.append((weights.astype(BF16), norm, scale))
    return results, peak


def sum_all(results, values, per):
    norm = value = None
    for index, ((weights, total, scale), v) in enumerate(zip(results, values)):
        if total is None:
            v = jnp.concatenate([v, jnp.ones_like(v)], axis=1)
        summed = jnp.dot(weights, v, preferred_element_type=F32)
        if total is None:
            summed, total = summed[:, :HEAD_DIM], summed[:, HEAD_DIM:]
        if scale is not None:
            total = total + scale * twice(norm, per)
            summed = summed + scale * twice(value, per)
        norm, value = total, summed
    return norm, value


def pool_kernel(
    k_hbm, v_hbm, k0, v0, k1, v1, k2, v2, k3, v3, kv4, kv5, kv6, kv7, kv8, sems
):
    groups = k0.shape[0] // GROUP
    sides = ((k_hbm, k0, k1, k2, k3), (v_hbm, v0, v1, v2, v3))

    def copy(index, group):
        rows = pl.ds(group * GROUP, GROUP)
        return pltpu.make_async_copy(sides[index][0].at[rows], sides[index][1].at[rows], sems.at[index, group])

    for group in range(groups):
        for index in range(2):
            copy(index, group).start()
    matrix = jnp.concatenate([averaging((1, 2, 3, 4), GROUP), jnp.zeros((16, GROUP), BF16)], axis=0)
    for first in range(0, groups, TOGETHER):
        here = range(first, first + TOGETHER)
        for group in here:
            for index in range(2):
                copy(index, group).wait()
        for group in here:
            for index, (_, o0, o1, o2, o3) in enumerate(sides):
                rows = o0[group * GROUP : (group + 1) * GROUP]
                pooled = jnp.dot(matrix, rows, preferred_element_type=F32).astype(BF16)
                o1[group * 128 : group * 128 + 128] = pooled[:128]
                o2[group * 64 : group * 64 + 64] = pooled[128:192]
                o3[group * 32 : group * 32 + 32] = pooled[192:224]
                kv4[index, group * 16 : group * 16 + 16] = pooled[224:240]
    matrix = jnp.concatenate([averaging((1, 2, 3, 4), BLOCK), jnp.zeros((8, BLOCK), BF16)], axis=0)
    for index in range(2):
        pooled = jnp.dot(matrix, kv4[index], preferred_element_type=F32).astype(BF16)
        kv5[index] = pooled[:64]
        kv6[index] = pooled[64:96]
        kv7[index] = pooled[96:112]
        kv8[index] = pooled[112:128]


def pool(keys, values):
    rows, width = keys.shape
    shapes = [pltpu.VMEM((rows >> level, width), BF16) for level in range(4) for _ in range(2)]
    shapes += [jax.ShapeDtypeStruct((2, count, width), BF16) for count in (128, 64, 32, 16, 16)]
    return pl.pallas_call(
        pool_kernel,
        in_specs=[pl.BlockSpec(memory_space=pl.ANY)] * 2,
        out_specs=[pl.BlockSpec(memory_space=pltpu.VMEM)] * len(shapes),
        out_shape=shapes,
        scratch_shapes=[pltpu.SemaphoreType.DMA((2, rows // GROUP))],
        compiler_params=pltpu.CompilerParams(vmem_limit_bytes=28 * MIB),
        cost_estimate=pl.CostEstimate(flops=2 * 2 * rows * GROUP * width, bytes_accessed=8 * MIB, transcendentals=0),
        name="pool",
    )(pltpu.with_memory_space_constraint(keys, pltpu.HBM), pltpu.with_memory_space_constraint(values, pltpu.HBM))


def near_kernel(start, q_ref, k0, v0, k1, v1, k2, v2, k3, v3, att_ref, log_ref, q4_ref):
    perm = slab_order(GROUP, 16)
    heads = [slice(c, c + HEAD_DIM) for c in range(0, q_ref.shape[1], HEAD_DIM)]
    lane = iota2((GROUP, HEAD_DIM), 1)

    def at(index, count):
        return pl.ds(pl.multiple_of(index * count, count), count)

    @pl.loop(0, att_ref.shape[0] // GROUP)
    def _(step):
        group = start + step
        level = jnp.dot(perm, q_ref[at(group, GROUP), :], preferred_element_type=F32)
        queries = [level.astype(BF16)]
        for _ in range(4):
            queries.insert(0, halve_slabs(level, 16).astype(BF16))
            level = queries[0].astype(F32)
        q4_ref[at(step, 16), :] = queries.pop(0)
        places = [at((group >> level) ^ 1, BLOCK) for level in (2, 1, 0)] + [at(group, GROUP)]
        keys, values = (
            [[ref[place, cols] for ref, place in zip(refs, places)] for cols in heads]
            for refs in ((k3, k2, k1, k0), (v3, v2, v1, v0))
        )
        scores = [score_all([q[:, cols] for q in queries], keys[head]) for head, cols in enumerate(heads)]
        weighed = [weigh_all(levels, 16) for levels in scores]
        logs = jnp.zeros((GROUP, HEAD_DIM), F32)
        for head, cols in enumerate(heads):
            results, peak = weighed[head]
            norm, value = sum_all(results, values[head], 16)
            att_ref[at(step, GROUP), cols] = (value * (1.0 / norm)).astype(BF16)
            logs = jnp.where(lane == head, peak * LOG2_SCALE + jnp.log2(norm), logs)
        log_ref[at(step, GROUP), :] = logs


def near(queries, pooled, start, count):
    width = queries.shape[1]
    return pl.pallas_call(
        functools.partial(near_kernel, start),
        in_specs=[pl.BlockSpec(memory_space=pltpu.VMEM)] * 9,
        out_specs=[pl.BlockSpec(memory_space=pltpu.VMEM)] * 3,
        out_shape=[
            pltpu.VMEM((count * GROUP, width), BF16),
            pltpu.VMEM((count * GROUP, HEAD_DIM), F32),
            pltpu.VMEM((count * 16, width), BF16),
        ],
        compiler_params=pltpu.CompilerParams(vmem_limit_bytes=28 * MIB),
        cost_estimate=pl.CostEstimate(
            flops=count * 8 * 2 * 2 * GROUP * GROUP * 256, bytes_accessed=count * 3 * MIB, transcendentals=count * 8 * 98304
        ),
        name="near",
    )(queries, *pooled)


def far_kernel(s4, *rest):
    sides, rest = (rest[:5], rest[5:10]), rest[10:]
    parts, (att_ref, sq_ref, coarse, coarse_log) = rest[:-4], rest[-4:]
    near_refs, log_refs, q4_refs = parts[0::3], parts[1::3], parts[2::3]
    heads = [slice(c, c + HEAD_DIM) for c in range(0, att_ref.shape[1], HEAD_DIM)]

    def coarse_levels():
        q4 = jnp.concatenate([ref[...] for ref in q4_refs], axis=0)
        level = jnp.dot(slab_order(BLOCK, 16), q4, preferred_element_type=F32)
        queries = [level.astype(BF16)]
        for _ in range(4):
            queries.insert(0, halve_slabs(level, 8).astype(BF16))
            level = queries[0].astype(F32)
        pieces = [[], [], [], [], [(s4, 0, 128)]]
        for l5, x_own, y2, y4, y6 in sides:
            along_x = [(x_own, 0), (y2, 0), (y4, 32), (y6, 32)]
            pieces[0] += [(ref, lo + 16, lo + 32) for ref, lo in along_x]
            pieces[1] += [(ref, lo, lo + 16) for ref, lo in along_x]
            pieces[2] += [(y4, 0, 32), (y6, 0, 32)]
            pieces[3] += [(l5, 0, 64)]
        keys, values = (
            [jnp.concatenate([ref[part, lo:hi, :] for ref, lo, hi in level], axis=0) for level in pieces]
            for part in (0, 1)
        )
        scores = [score_all([q[:, cols] for q in queries], [k[:, cols] for k in keys]) for cols in heads]
        weighed = [weigh_all(levels, 8) for levels in scores]
        lane = iota2((BLOCK, HEAD_DIM), 1)
        logs = jnp.zeros((BLOCK, HEAD_DIM), F32)
        for head, cols in enumerate(heads):
            results, peak = weighed[head]
            norm, value = sum_all(results, [v[:, cols] for v in values], 8)
            value = value * (1.0 / norm)
            for slab in range(16):
                coarse[head, pl.ds(slab, 8, stride=16), :] = value[slab * 8 : slab * 8 + 8]
            logs = jnp.where(lane == head, peak * LOG2_SCALE + jnp.log2(norm) + 4.0, logs)
        for slab in range(16):
            coarse_log[pl.ds(slab, 8, stride=16), :] = logs[slab * 8 : slab * 8 + 8]

    def merge(near_ref, log_ref, first, step):
        def at(index, count):
            return slice(index * count, (index + 1) * count)

        group = first + step
        gap = log_ref[at(step, GROUP), :].reshape(16, 16, HEAD_DIM) - coarse_log[at(group, 16), :][None]
        share = (1.0 / (1.0 + jnp.exp2(gap))).reshape(GROUP, HEAD_DIM)
        squares = jnp.zeros((GROUP, HEAD_DIM), F32)
        for head, cols in enumerate(heads):
            part = near_ref[at(step, GROUP), cols].astype(F32)
            delta = (coarse[head, at(group, 16), :][None] - part.reshape(16, 16, HEAD_DIM)).reshape(GROUP, HEAD_DIM)
            attended = part + share[:, head : head + 1] * delta
            squares = squares + attended * attended
            att_ref[at(group, GROUP), cols] = attended.astype(BF16)
        high = squares.astype(BF16)
        low = (squares - high.astype(F32)).astype(BF16)
        ones = jnp.ones((16, 2 * HEAD_DIM), BF16)
        pair = jnp.concatenate([high, low], axis=1)
        sums = lax.dot_general(ones, pair, NT, preferred_element_type=F32)
        sq_ref[group : group + 1] = sums[:1]

    coarse_levels()
    first = 0
    for near_ref, log_ref in zip(near_refs, log_refs):
        count = near_ref.shape[0] // GROUP
        for step in range(count):
            merge(near_ref, log_ref, first, step)
        first += count


def far(s4, own, other, parts):
    operands = [s4, *own, *other, *[array for part in parts for array in part]]
    rows, width = sum(part[0].shape[0] for part in parts), s4.shape[2]
    whole = pl.BlockSpec(memory_space=pltpu.VMEM)
    return pl.pallas_call(
        far_kernel,
        in_specs=[whole] * len(operands),
        out_specs=[whole, whole],
        out_shape=[pltpu.VMEM((rows, width), BF16), jax.ShapeDtypeStruct((rows // GROUP, GROUP), F32)],
        scratch_shapes=[pltpu.VMEM((width // HEAD_DIM, BLOCK, HEAD_DIM), F32), pltpu.VMEM((BLOCK, HEAD_DIM), F32)],
        compiler_params=pltpu.CompilerParams(vmem_limit_bytes=28 * MIB),
        name="far",
    )(*operands)


def norm_kernel(features, att_ref, s0, s1, s2, s3, gain_ref, out_hbm, out_vmem, sems):
    shape = (GROUP, GROUP)
    source = (iota2(shape, 0) % 16) * 16 + iota2(shape, 0) // 16
    hit = iota2(shape, 1) == source
    scale = lax.rsqrt(((s0[...] + s1[...]) + (s2[...] + s3[...])) / features + 1e-06)
    copies = []
    for group in range(att_ref.shape[0] // GROUP):
        rows = pl.ds(group * GROUP, GROUP)
        matrix = jnp.where(hit, scale[group : group + 1], 0.0).astype(BF16)
        mixed = jnp.dot(matrix, att_ref[rows, :], preferred_element_type=F32)
        out_vmem[rows, :] = (mixed * gain_ref[...]).astype(BF16)
        copies.append(pltpu.make_async_copy(out_vmem.at[rows], out_hbm.at[rows], sems.at[group]))
        copies[-1].start()
    for copy in copies:
        copy.wait()


def normed(att, sums, gain, features):
    rows, width = att.shape
    whole = pl.BlockSpec(memory_space=pltpu.VMEM)
    return pl.pallas_call(
        functools.partial(norm_kernel, features),
        in_specs=[whole] * 6,
        out_specs=pl.BlockSpec(memory_space=pl.ANY),
        out_shape=jax.ShapeDtypeStruct((rows, width), BF16),
        scratch_shapes=[pltpu.VMEM((rows, width), BF16), pltpu.SemaphoreType.DMA((rows // GROUP,))],
        compiler_params=pltpu.CompilerParams(vmem_limit_bytes=28 * MIB),
        name="norm",
    )(att, *sums, gain.reshape(1, width))


def swapped(array, axis, bits):
    return lax.ppermute(array, axis, [(i, i ^ bits) for i in range(lax.axis_size(axis))])


def local(queries, keys, values, gain):
    *pooled, kv4, kv5, kv6, kv7, kv8 = pool(keys, values)
    queries, kv7, kv8 = lax.optimization_barrier((queries, kv7, kv8))
    rows8 = kv8[:, :8]
    x7 = swapped(kv7, "seq", 8)
    x8a = swapped(rows8, "seq", 16)
    x8b = swapped(rows8, "seq", 24)
    l5 = swapped(kv5, "seq", 2)
    s4 = swapped(kv4, "seq", 1)
    first = near(queries, pooled, 0, SPLIT[0])
    x7, x8a, x8b, first = lax.optimization_barrier((x7, x8a, x8b, first))
    x_own = jnp.concatenate([x7, x8a, x8b], axis=1)
    both = jnp.concatenate([kv6, x_own], axis=1)
    early = [l5, x_own]
    own = [swapped(x_own, "seq", 2), swapped(both, "seq", 4), swapped(both, "seq", 6)]
    early_other = [swapped(a, "seq", 1) for a in early]
    second = near(queries, pooled, SPLIT[0], SPLIT[1])
    own, second = lax.optimization_barrier((own, second))
    other = [swapped(a, "seq", 1) for a in own]
    third = near(queries, pooled, SPLIT[0] + SPLIT[1], SPLIT[2])
    att, squares = far(s4, early + own, early_other + other, (first, second, third))
    sums = [squares] + [
        lax.ppermute(squares, "head", [(i, (i + s) % 4) for i in range(4)]) for s in (1, 2, 3)
    ]
    return normed(att, sums, gain, lax.axis_size("head") * queries.shape[1])


def solution(mesh):
    return jax.shard_map(
        local,
        mesh=mesh,
        in_specs=(P("seq", "head"), P("seq", "head"), P("seq", "head"), P("head")),
        out_specs=P("seq", "head"),
        check_vma=False,
    )
```

```python
import functools
import math

import jax
import jax.numpy as jnp
from jax import lax
from jax.experimental import pallas as pl
from jax.experimental.pallas import tpu as pltpu
from jax.sharding import PartitionSpec as P

HEAD_DIM = 128
BLOCK = 128
GROUP = 256
LOG2_SCALE = math.log2(math.e) / math.sqrt(HEAD_DIM)
F32 = jnp.float32
BF16 = jnp.bfloat16
NT = (((1,), (1,)), ((), ()))
MIB = 1 << 20
SPLIT = (2, 5, 1)
TOGETHER = 2


def iota2(shape, dim):
    return lax.broadcasted_iota(jnp.int32, shape, dim)


def averaging(levels, width):
    parts = []
    for level in levels:
        shape = (width >> level, width)
        hit = (iota2(shape, 1) >> level) == iota2(shape, 0)
        parts.append(jnp.where(hit, 2.0**-level, 0.0))
    return jnp.concatenate(parts, axis=0).astype(BF16)


def slab_order(rows, slabs):
    shape = (rows, rows)
    per = rows // slabs
    row = iota2(shape, 0)
    source = (row & (per - 1)) * slabs + (row >> (per.bit_length() - 1))
    return jnp.where(iota2(shape, 1) == source, 1.0, 0.0).astype(BF16)


def twice(array, per):
    count, width = array.shape[0] // per, array.shape[1]
    wide = jnp.broadcast_to(array.reshape(count, 1, per, width), (count, 2, per, width))
    return wide.reshape(2 * count * per, width)


def halve_slabs(array, per):
    count, width = array.shape[0] // (2 * per), array.shape[1]
    pairs = array.reshape(count, 2, per, width)
    return ((pairs[:, 0] + pairs[:, 1]) * 0.5).reshape(count * per, width)


def score_all(queries, keys):
    return [lax.dot_general(q, k, NT, preferred_element_type=F32) for q, k in zip(queries, keys)]


def weigh_all(scores, per):
    results, peak = [], None
    for index, level in enumerate(scores):
        own, scale = jnp.max(level, axis=1, keepdims=True), None
        if peak is not None:
            coarse = twice(peak, per)
            own = jnp.maximum(own, coarse)
            scale = 2.0 * jnp.exp2((coarse - own) * LOG2_SCALE)
        peak = own
        weights = jnp.exp2((level - peak) * LOG2_SCALE)
        norm = None if index + 1 == len(scores) else jnp.sum(weights, axis=1, keepdims=True)
        results.append((weights.astype(BF16), norm, scale))
    return results, peak


def sum_all(results, values, per):
    norm = value = None
    for index, ((weights, total, scale), v) in enumerate(zip(results, values)):
        if total is None:
            v = jnp.concatenate([v, jnp.ones_like(v)], axis=1)
        summed = jnp.dot(weights, v, preferred_element_type=F32)
        if total is None:
            summed, total = summed[:, :HEAD_DIM], summed[:, HEAD_DIM:]
        if scale is not None:
            total = total + scale * twice(norm, per)
            summed = summed + scale * twice(value, per)
        norm, value = total, summed
    return norm, value


def pool_kernel(
    k_hbm, v_hbm, k0, v0, k1, v1, k2, v2, k3, v3, kv4, kv5, kv6, kv7, kv8, sems
):
    groups = k0.shape[0] // GROUP
    sides = ((k_hbm, k0, k1, k2, k3), (v_hbm, v0, v1, v2, v3))

    def copy(index, group):
        rows = pl.ds(group * GROUP, GROUP)
        return pltpu.make_async_copy(sides[index][0].at[rows], sides[index][1].at[rows], sems.at[index, group])

    for group in range(groups):
        for index in range(2):
            copy(index, group).start()
    matrix = jnp.concatenate([averaging((1, 2, 3, 4), GROUP), jnp.zeros((16, GROUP), BF16)], axis=0)
    for first in range(0, groups, TOGETHER):
        here = range(first, first + TOGETHER)
        for group in here:
            for index in range(2):
                copy(index, group).wait()
        for group in here:
            for index, (_, o0, o1, o2, o3) in enumerate(sides):
                rows = o0[group * GROUP : (group + 1) * GROUP]
                pooled = jnp.dot(matrix, rows, preferred_element_type=F32).astype(BF16)
                o1[group * 128 : group * 128 + 128] = pooled[:128]
                o2[group * 64 : group * 64 + 64] = pooled[128:192]
                o3[group * 32 : group * 32 + 32] = pooled[192:224]
                kv4[index, group * 16 : group * 16 + 16] = pooled[224:240]
    matrix = jnp.concatenate([averaging((1, 2, 3, 4), BLOCK), jnp.zeros((8, BLOCK), BF16)], axis=0)
    for index in range(2):
        pooled = jnp.dot(matrix, kv4[index], preferred_element_type=F32).astype(BF16)
        kv5[index] = pooled[:64]
        kv6[index] = pooled[64:96]
        kv7[index] = pooled[96:112]
        kv8[index] = pooled[112:128]


def pool(keys, values):
    rows, width = keys.shape
    shapes = [pltpu.VMEM((rows >> level, width), BF16) for level in range(4) for _ in range(2)]
    shapes += [jax.ShapeDtypeStruct((2, count, width), BF16) for count in (128, 64, 32, 16, 16)]
    return pl.pallas_call(
        pool_kernel,
        in_specs=[pl.BlockSpec(memory_space=pl.ANY)] * 2,
        out_specs=[pl.BlockSpec(memory_space=pltpu.VMEM)] * len(shapes),
        out_shape=shapes,
        scratch_shapes=[pltpu.SemaphoreType.DMA((2, rows // GROUP))],
        compiler_params=pltpu.CompilerParams(vmem_limit_bytes=28 * MIB),
        cost_estimate=pl.CostEstimate(flops=2 * 2 * rows * GROUP * width, bytes_accessed=8 * MIB, transcendentals=0),
        name="pool",
    )(pltpu.with_memory_space_constraint(keys, pltpu.HBM), pltpu.with_memory_space_constraint(values, pltpu.HBM))


def near_kernel(start, q_ref, k0, v0, k1, v1, k2, v2, k3, v3, att_ref, log_ref, q4_ref):
    perm = slab_order(GROUP, 16)
    heads = [slice(c, c + HEAD_DIM) for c in range(0, q_ref.shape[1], HEAD_DIM)]
    lane = iota2((GROUP, HEAD_DIM), 1)

    def at(index, count):
        return pl.ds(pl.multiple_of(index * count, count), count)

    @pl.loop(0, att_ref.shape[0] // GROUP)
    def _(step):
        group = start + step
        level = jnp.dot(perm, q_ref[at(group, GROUP), :], preferred_element_type=F32)
        queries = [level.astype(BF16)]
        for _ in range(4):
            queries.insert(0, halve_slabs(level, 16).astype(BF16))
            level = queries[0].astype(F32)
        q4_ref[at(step, 16), :] = queries.pop(0)
        places = [at((group >> level) ^ 1, BLOCK) for level in (2, 1, 0)] + [at(group, GROUP)]
        keys, values = (
            [[ref[place, cols] for ref, place in zip(refs, places)] for cols in heads]
            for refs in ((k3, k2, k1, k0), (v3, v2, v1, v0))
        )
        scores = [score_all([q[:, cols] for q in queries], keys[head]) for head, cols in enumerate(heads)]
        weighed = [weigh_all(levels, 16) for levels in scores]
        logs = jnp.zeros((GROUP, HEAD_DIM), F32)
        for head, cols in enumerate(heads):
            results, peak = weighed[head]
            norm, value = sum_all(results, values[head], 16)
            att_ref[at(step, GROUP), cols] = (value * (1.0 / norm)).astype(BF16)
            logs = jnp.where(lane == head, peak * LOG2_SCALE + jnp.log2(norm), logs)
        log_ref[at(step, GROUP), :] = logs


def near(queries, pooled, start, count):
    width = queries.shape[1]
    return pl.pallas_call(
        functools.partial(near_kernel, start),
        in_specs=[pl.BlockSpec(memory_space=pltpu.VMEM)] * 9,
        out_specs=[pl.BlockSpec(memory_space=pltpu.VMEM)] * 3,
        out_shape=[
            pltpu.VMEM((count * GROUP, width), BF16),
            pltpu.VMEM((count * GROUP, HEAD_DIM), F32),
            pltpu.VMEM((count * 16, width), BF16),
        ],
        compiler_params=pltpu.CompilerParams(vmem_limit_bytes=28 * MIB),
        cost_estimate=pl.CostEstimate(
            flops=count * 8 * 2 * 2 * GROUP * GROUP * 256, bytes_accessed=count * 3 * MIB, transcendentals=count * 8 * 98304
        ),
        name="near",
    )(queries, *pooled)


def far_kernel(s4, *rest):
    sides, rest = (rest[:5], rest[5:10]), rest[10:]
    parts, (att_ref, sq_ref, coarse, coarse_log) = rest[:-4], rest[-4:]
    near_refs, log_refs, q4_refs = parts[0::3], parts[1::3], parts[2::3]
    heads = [slice(c, c + HEAD_DIM) for c in range(0, att_ref.shape[1], HEAD_DIM)]

    def coarse_levels():
        q4 = jnp.concatenate([ref[...] for ref in q4_refs], axis=0)
        level = jnp.dot(slab_order(BLOCK, 16), q4, preferred_element_type=F32)
        queries = [level.astype(BF16)]
        for _ in range(4):
            queries.insert(0, halve_slabs(level, 8).astype(BF16))
            level = queries[0].astype(F32)
        pieces = [[], [], [], [], [(s4, 0, 128)]]
        for l5, x_own, y2, y4, y6 in sides:
            along_x = [(x_own, 0), (y2, 0), (y4, 32), (y6, 32)]
            pieces[0] += [(ref, lo + 16, lo + 32) for ref, lo in along_x]
            pieces[1] += [(ref, lo, lo + 16) for ref, lo in along_x]
            pieces[2] += [(y4, 0, 32), (y6, 0, 32)]
            pieces[3] += [(l5, 0, 64)]
        keys, values = (
            [jnp.concatenate([ref[part, lo:hi, :] for ref, lo, hi in level], axis=0) for level in pieces]
            for part in (0, 1)
        )
        scores = [score_all([q[:, cols] for q in queries], [k[:, cols] for k in keys]) for cols in heads]
        weighed = [weigh_all(levels, 8) for levels in scores]
        lane = iota2((BLOCK, HEAD_DIM), 1)
        logs = jnp.zeros((BLOCK, HEAD_DIM), F32)
        for head, cols in enumerate(heads):
            results, peak = weighed[head]
            norm, value = sum_all(results, [v[:, cols] for v in values], 8)
            value = value * (1.0 / norm)
            for slab in range(16):
                coarse[head, pl.ds(slab, 8, stride=16), :] = value[slab * 8 : slab * 8 + 8]
            logs = jnp.where(lane == head, peak * LOG2_SCALE + jnp.log2(norm) + 4.0, logs)
        for slab in range(16):
            coarse_log[pl.ds(slab, 8, stride=16), :] = logs[slab * 8 : slab * 8 + 8]

    def merge(near_ref, log_ref, first, step):
        def at(index, count):
            return slice(index * count, (index + 1) * count)

        group = first + step
        gap = log_ref[at(step, GROUP), :].reshape(16, 16, HEAD_DIM) - coarse_log[at(group, 16), :][None]
        share = (1.0 / (1.0 + jnp.exp2(gap))).reshape(GROUP, HEAD_DIM)
        squares = jnp.zeros((GROUP, HEAD_DIM), F32)
        for head, cols in enumerate(heads):
            part = near_ref[at(step, GROUP), cols].astype(F32)
            delta = (coarse[head, at(group, 16), :][None] - part.reshape(16, 16, HEAD_DIM)).reshape(GROUP, HEAD_DIM)
            attended = part + share[:, head : head + 1] * delta
            squares = squares + attended * attended
            att_ref[at(group, GROUP), cols] = attended.astype(BF16)
        high = squares.astype(BF16)
        low = (squares - high.astype(F32)).astype(BF16)
        ones = jnp.ones((16, 2 * HEAD_DIM), BF16)
        pair = jnp.concatenate([high, low], axis=1)
        sums = lax.dot_general(ones, pair, NT, preferred_element_type=F32)
        sq_ref[group : group + 1] = sums[:1]

    coarse_levels()
    first = 0
    for near_ref, log_ref in zip(near_refs, log_refs):
        count = near_ref.shape[0] // GROUP
        for step in range(count):
            merge(near_ref, log_ref, first, step)
        first += count


def far(s4, own, other, parts):
    operands = [s4, *own, *other, *[array for part in parts for array in part]]
    rows, width = sum(part[0].shape[0] for part in parts), s4.shape[2]
    whole = pl.BlockSpec(memory_space=pltpu.VMEM)
    return pl.pallas_call(
        far_kernel,
        in_specs=[whole] * len(operands),
        out_specs=[whole, whole],
        out_shape=[pltpu.VMEM((rows, width), BF16), jax.ShapeDtypeStruct((rows // GROUP, GROUP), F32)],
        scratch_shapes=[pltpu.VMEM((width // HEAD_DIM, BLOCK, HEAD_DIM), F32), pltpu.VMEM((BLOCK, HEAD_DIM), F32)],
        compiler_params=pltpu.CompilerParams(vmem_limit_bytes=28 * MIB),
        name="far",
    )(*operands)


def norm_kernel(features, att_ref, s0, s1, s2, s3, gain_ref, out_hbm, out_vmem, sems):
    shape = (GROUP, GROUP)
    source = (iota2(shape, 0) & 15) * 16 + (iota2(shape, 0) >> 4)
    hit = iota2(shape, 1) == source
    scale = lax.rsqrt(((s0[...] + s1[...]) + (s2[...] + s3[...])) / features + 1e-06)
    copies = []
    for first in range(0, att_ref.shape[0] // GROUP, TOGETHER):
        for group in range(first, first + TOGETHER):
            rows = pl.ds(group * GROUP, GROUP)
            matrix = jnp.where(hit, scale[group : group + 1], 0.0).astype(BF16)
            mixed = jnp.dot(matrix, att_ref[rows, :], preferred_element_type=F32)
            out_vmem[rows, :] = (mixed * gain_ref[...]).astype(BF16)
        for group in range(first, first + TOGETHER):
            rows = pl.ds(group * GROUP, GROUP)
            copies.append(pltpu.make_async_copy(out_vmem.at[rows], out_hbm.at[rows], sems.at[group]))
            copies[-1].start()
    for copy in copies:
        copy.wait()


def normed(att, sums, gain, features):
    rows, width = att.shape
    whole = pl.BlockSpec(memory_space=pltpu.VMEM)
    return pl.pallas_call(
        functools.partial(norm_kernel, features),
        in_specs=[whole] * 6,
        out_specs=pl.BlockSpec(memory_space=pl.ANY),
        out_shape=jax.ShapeDtypeStruct((rows, width), BF16),
        scratch_shapes=[pltpu.VMEM((rows, width), BF16), pltpu.SemaphoreType.DMA((rows // GROUP,))],
        compiler_params=pltpu.CompilerParams(vmem_limit_bytes=28 * MIB),
        name="norm",
    )(att, *sums, gain.reshape(1, width))


def swapped(array, axis, bits):
    return lax.ppermute(array, axis, [(i, i ^ bits) for i in range(lax.axis_size(axis))])


def local(queries, keys, values, gain):
    *pooled, kv4, kv5, kv6, kv7, kv8 = pool(keys, values)
    queries, kv7, kv8 = lax.optimization_barrier((queries, kv7, kv8))
    rows8 = kv8[:, :8]
    x7 = swapped(kv7, "seq", 8)
    x8a = swapped(rows8, "seq", 16)
    x8b = swapped(rows8, "seq", 24)
    l5 = swapped(kv5, "seq", 2)
    s4 = swapped(kv4, "seq", 1)
    first = near(queries, pooled, 0, SPLIT[0])
    x7, x8a, x8b, first = lax.optimization_barrier((x7, x8a, x8b, first))
    x_own = jnp.concatenate([x7, x8a, x8b], axis=1)
    both = jnp.concatenate([kv6, x_own], axis=1)
    early = [l5, x_own]
    own = [swapped(x_own, "seq", 2), swapped(both, "seq", 4), swapped(both, "seq", 6)]
    early_other = [swapped(a, "seq", 1) for a in early]
    second = near(queries, pooled, SPLIT[0], SPLIT[1])
    own, second = lax.optimization_barrier((own, second))
    other = [swapped(a, "seq", 1) for a in own]
    third = near(queries, pooled, SPLIT[0] + SPLIT[1], SPLIT[2])
    att, squares = far(s4, early + own, early_other + other, (first, second, third))
    sums = [squares] + [
        lax.ppermute(squares, "head", [(i, (i + s) % 4) for i in range(4)]) for s in (1, 2, 3)
    ]
    return normed(att, sums, gain, lax.axis_size("head") * queries.shape[1])


def solution(mesh):
    return jax.shard_map(
        local,
        mesh=mesh,
        in_specs=(P("seq", "head"), P("seq", "head"), P("seq", "head"), P("head")),
        out_specs=P("seq", "head"),
        check_vma=False,
    )
```
